32 devices in a mesh: slab: 2 (over y), tile: 4 (over z), view: 4 (over x, core).
Axes of the slice: x: 2, y: 2, z: 4, core: 2. Of those that a mesh axis runs over, the one named last changes fastest.
Arguments:
- recorded: float32 [4, 96, 32, 1024], P('view', 'tile', 'slab'), parts along dimension 2, may hold values from 0.5 to 2
- psf_taps: float32 [4, 3, 15], P('view'), may hold values from 0.2 to 1
- estimate: float32 [96, 32, 1024], P('tile', 'slab'), parts along dimension 1, may hold values from 0.5 to 2
Outputs:
- joined: float32 [96, 32, 1024], P('tile', 'slab'), parts along dimension 1
The draws below stay inside these ranges and needn't reach their ends.
There are 2 independent parts, one for each index of `slab`. The reference program is written for one: setup_inputs(seed, part) draws one part's arguments, and reference() takes and returns one part's arrays. A program takes and returns all parts, laid end to end along the dimension named above; an argument that names none is the same for every part. Nothing has to cross between parts.
All inputs are finite; a program needn't handle non-finite values.
Results may differ from the reference program's by a relative error of at most 0.00002.
Values sent between devices are 32-bit elements; how exact they have to be, the bound alone decides.
A program may use at most 64 MiB of HBM per device.

```python
import math
import jax
import jax.numpy as jnp
from jax import lax

NZ = 16
NY = 1024
RADIUS = 7
ITERS = 2
TAPS = 15
VIEWS = 4
NX = 96


def steps_of(key, extent, split, smallest, top_value):
    loudness = 1.0
    for position, shards_of in split:
        steps = jax.random.uniform(jax.random.fold_in(jax.random.fold_in(key, 6), position), (shards_of,), jnp.float32, smallest / len(split), top_value / len(split))
        loudness = loudness * jnp.repeat(jnp.exp(steps), extent[position] // shards_of).reshape((-1,) + (1,) * (len(extent) - 1 - position))
    return loudness


def setup_inputs(seed: int = 0, part: int = 0) -> dict:
    streams_of = jax.random.split(jax.random.key(seed), 4)
    part_keys = jax.random.split(jax.random.fold_in(streams_of[3], part), 4)
    recorded = jnp.clip(0.5 + 1.5 * jax.random.uniform(part_keys[0], (VIEWS, NX, NZ, NY), jnp.float32) ** steps_of(part_keys[0], (VIEWS, NX, NZ, NY), ((0, 4), (1, 4)), -0.2, 0.2), 0.5, 2.0)
    psf_taps = jnp.clip(jnp.exp(math.log(1.0) - 1.609438 * jax.random.uniform(streams_of[1], (VIEWS, 3, TAPS), jnp.float32) ** steps_of(streams_of[1], (VIEWS, 3, TAPS), ((0, 4),), -0.2, 0.2)), 0.2, 1.0)
    estimate = jnp.clip(0.5 + 1.5 * jax.random.uniform(part_keys[2], (NX, NZ, NY), jnp.float32) ** steps_of(part_keys[2], (NX, NZ, NY), ((0, 4),), -0.2, 0.2), 0.5, 2.0)
    return dict(recorded=recorded, psf_taps=psf_taps, estimate=estimate)


def valid_along(padded, kernel_row, axis_num, mirrored):
    length_out = padded.shape[axis_num] - 2 * RADIUS
    summed = jnp.zeros(padded.shape[:axis_num] + (length_out,) + padded.shape[axis_num + 1:], jnp.float32)
    for offset in range(2 * RADIUS + 1):
        weight = kernel_row[2 * RADIUS - offset] if mirrored else kernel_row[offset]
        summed = summed + weight * lax.slice_in_dim(padded, offset, offset + length_out, axis=axis_num)
    return summed


def along(values_in, kernel_row, axis_num, mirrored):
    widths = [(0, 0)] * values_in.ndim
    widths[axis_num] = (RADIUS, RADIUS)
    return valid_along(jnp.pad(values_in, widths), kernel_row, axis_num, mirrored)


def blur(values_in, kernel_view, mirrored):
    result = along(values_in, kernel_view[0], 0, mirrored)
    result = along(result, kernel_view[1], 1, mirrored)
    return along(result, kernel_view[2], 2, mirrored)


def reference(recorded, psf_taps, estimate):
    kernel = psf_taps / jnp.sum(psf_taps, axis=2, keepdims=True)
    for iteration in range(ITERS):
        log_total = jnp.zeros(estimate.shape, jnp.float32)
        for view_num in range(VIEWS):
            blurred = blur(estimate, kernel[view_num], False)
            quotient = recorded[view_num] / blurred
            correction = blur(quotient, kernel[view_num], True)
            log_total = log_total + jnp.log(correction)
        estimate = estimate * jnp.exp(log_total / VIEWS)
    return estimate
```

```python
import functools

import jax
import jax.numpy as jnp
from jax import lax
from jax.experimental import pallas as pl
from jax.experimental.pallas import tpu as pltpu
from jax.sharding import PartitionSpec as P

RADIUS = 7
TAPS = 2 * RADIUS + 1
ITERS = 2
LANE = 128
CORES = 2
F32 = jnp.float32
BF16 = jnp.bfloat16
MESH = pl.DeviceIdType.MESH


def split(value):
    hi = value.astype(BF16)
    return hi, (value - hi.astype(F32)).astype(BF16)


def dot(a, b):
    return jnp.dot(a, b, preferred_element_type=F32)


def pieces(total, size):
    return [(start, min(size, total - start)) for start in range(0, total, size)]


def window_of(chip, chips, ny):
    part = ny // chips
    width = part + LANE * min(chips - 1, 2)
    start = jnp.clip(chip * part - LANE, 0, ny - width)
    return pl.multiple_of(start, LANE), width


def body(
    nx, nz, ny, tiles, views,
    rec_ref, taps_ref, est_ref, out_ref,
    est_x, quo_x, rec_in, acc, acc_in, kern, mat_xz, mat_y, u_hi, u_lo,
    kern_send, kern_recv, rec_send, rec_recv, rim_send, rim_recv,
    acc_send, acc_recv, out_send, out_recv, fwd_send, fwd_recv,
):
    chips = views // CORES
    part = ny // chips
    rows = nx * nz
    rim = RADIUS * nz
    half = rows // 2
    tile = lax.axis_index("tile")
    view = lax.axis_index("view")
    chip, core = view // CORES, view % CORES
    mate = chip * CORES + (1 - core)
    start, width = window_of(chip, chips, ny)
    own = slice(rim, rim + rows)

    def chip_at(step):
        return lax.rem(chip + step, chips)

    def peer(step):
        return {"view": chip_at(step) * CORES + core}

    barrier = pltpu.get_barrier_semaphore()
    for step in range(1, chips):
        pl.semaphore_signal(barrier, inc=1, device_id=peer(step), device_id_type=MESH)
    pl.semaphore_signal(barrier, inc=1, device_id={"view": mate}, device_id_type=MESH)

    @pl.when(tile > 0)
    def _():
        pl.semaphore_signal(barrier, inc=1, device_id={"tile": tile - 1}, device_id_type=MESH)

    @pl.when(tile < tiles - 1)
    def _():
        pl.semaphore_signal(barrier, inc=1, device_id={"tile": tile + 1}, device_id_type=MESH)

    taps = taps_ref[...]
    kern[0, 0:3, 0:TAPS] = taps / jnp.sum(taps, axis=1, keepdims=True)
    est_x[own, :] = est_ref[:, pl.ds(start, width)]

    @pl.when(tile == 0)
    def _():
        est_x[0:rim, :] = jnp.zeros((rim, width), F32)
        for s in range(chips):
            quo_x[s, 0:rim, :] = jnp.zeros((rim, width), F32)

    @pl.when(tile == tiles - 1)
    def _():
        est_x[rim + rows :, :] = jnp.zeros((rim, width), F32)
        for s in range(chips):
            quo_x[s, rim + rows :, :] = jnp.zeros((rim, width), F32)

    tile_peers = jnp.minimum(tile, 1) + jnp.minimum(tiles - 1 - tile, 1)
    pl.semaphore_wait(barrier, chips + tile_peers)

    def rim_down(array, number):
        return pltpu.make_async_remote_copy(
            src_ref=array.at[pl.ds(rim, rim)],
            dst_ref=array.at[pl.ds(rim + rows, rim)],
            send_sem=rim_send.at[number, 0],
            recv_sem=rim_recv.at[number, 0],
            device_id={"tile": tile - 1},
            device_id_type=MESH,
        )

    def rim_up(array, number):
        return pltpu.make_async_remote_copy(
            src_ref=array.at[pl.ds(rows, rim)],
            dst_ref=array.at[pl.ds(0, rim)],
            send_sem=rim_send.at[number, 1],
            recv_sem=rim_recv.at[number, 1],
            device_id={"tile": tile + 1},
            device_id_type=MESH,
        )

    def rim_start(array, number, which):
        @pl.when(tile > 0 if which == 0 else tile < tiles - 1)
        def _():
            (rim_up if which else rim_down)(array, number).start()

    def rim_wait(array, number):
        @pl.when(tile > 0)
        def _():
            rim_down(array, number).wait_send()
            rim_up(array, number).wait_recv()

        @pl.when(tile < tiles - 1)
        def _():
            rim_up(array, number).wait_send()
            rim_down(array, number).wait_recv()

    row_parts = [(0, rim, 0), (rows - rim, rim, 1), (rim, rows - 2 * rim, None)]

    rim_start(est_x, 0, 0)
    rim_start(est_x, 0, 1)

    def kern_copy(step):
        return pltpu.make_async_remote_copy(
            src_ref=kern.at[0],
            dst_ref=kern.at[step],
            send_sem=kern_send.at[step],
            recv_sem=kern_recv.at[step],
            device_id=peer(chips - step),
            device_id_type=MESH,
        )

    def rec_copy(step, index):
        row, count, _ = row_parts[index]
        begin, _ = window_of(chip_at(chips - step), chips, ny)
        return pltpu.make_async_remote_copy(
            src_ref=rec_ref.at[pl.ds(row, count), pl.ds(begin, width)],
            dst_ref=rec_in.at[step, pl.ds(row, count)],
            send_sem=rec_send.at[step, index],
            recv_sem=rec_recv.at[step, index],
            device_id=peer(chips - step),
            device_id_type=MESH,
        )

    for step in range(1, chips):
        kern_copy(step).start()
        for index in range(len(row_parts)):
            rec_copy(step, index).start()

    def build(s):
        kern_s = kern[s]
        width_s = mat_xz.shape[-1]
        wide = -(-width_s // LANE) * LANE
        a = lax.broadcasted_iota(jnp.int32, (nz, wide), 0)
        column = lax.broadcasted_iota(jnp.int32, (nz, wide), 1)
        p, b = lax.div(column, jnp.int32(nz)), lax.rem(column, jnp.int32(nz))
        r = lax.broadcasted_iota(jnp.int32, (3 * LANE, LANE), 0)
        c = lax.broadcasted_iota(jnp.int32, (3 * LANE, LANE), 1)
        for mirrored in range(2):
            fx = jnp.zeros((nz, wide), F32)
            fz = jnp.zeros((nz, wide), F32)
            fy = jnp.zeros((3 * LANE, LANE), F32)
            for k in range(TAPS):
                o = TAPS - 1 - k if mirrored else k
                fx = jnp.where(p == k, kern_s[0:1, o : o + 1], fx)
                fz = jnp.where(b - a + RADIUS == k, kern_s[1:2, o : o + 1], fz)
                fy = jnp.where(r - c - LANE + RADIUS == k, kern_s[2:3, o : o + 1], fy)
            strip = fx * fz
            for i in range(nx // 2):
                moved = strip if i == 0 else pltpu.roll(strip, i * nz, 1)
                hi, lo = split(moved)
                mat_xz[s, mirrored, i * nz : (i + 1) * nz, :] = hi[:, :width_s]
                mat_xz[s, mirrored, half + i * nz : half + (i + 1) * nz, :] = lo[:, :width_s]
            for index, value in enumerate(split(fy)):
                mat_y[s, mirrored, index, 0 : 3 * LANE, 0:LANE] = value
                mat_y[s, mirrored, index, LANE : 4 * LANE, LANE : 2 * LANE] = value
                mat_y[s, mirrored, index, 3 * LANE :, 0:LANE] = jnp.zeros((LANE, LANE), BF16)
                mat_y[s, mirrored, index, 0:LANE, LANE : 2 * LANE] = jnp.zeros((LANE, LANE), BF16)

    for u in (u_hi, u_lo):
        u[:, 0:LANE] = jnp.zeros((rows, LANE), BF16)
        u[:, LANE + width :] = jnp.zeros((rows, LANE), BF16)

    def blur(source, s, mirrored, store):
        depth = half + 2 * rim
        for h in range(2):
            for c0, n in pieces(width, 2 * LANE):
                hi, lo = split(source[h * half : h * half + depth, c0 : c0 + n])
                both = dot(mat_xz[s, mirrored], hi)
                value = both[:half] + both[half:] + dot(mat_xz[s, mirrored, :half], lo)
                hi, lo = split(value)
                u_hi[h * half : (h + 1) * half, LANE + c0 : LANE + c0 + n] = hi
                u_lo[h * half : (h + 1) * half, LANE + c0 : LANE + c0 + n] = lo
        for c0, n in pieces(width, 2 * LANE):
            k = n + 2 * LANE
            hi, lo = u_hi[:, c0 : c0 + k], u_lo[:, c0 : c0 + k]
            m_hi, m_lo = mat_y[s, mirrored, 0, :k, :n], mat_y[s, mirrored, 1, :k, :n]
            store(c0, n, dot(hi, m_hi) + dot(lo, m_hi) + dot(hi, m_lo))

    build(0)
    for it in range(ITERS):
        rim_wait(est_x, 0)
        for s in range(chips):
            if it == 0 and s > 0:
                kern_copy(s).wait()
                build(s)
            quo = quo_x.at[s]

            def store_blurred(c0, n, value):
                quo[own, c0 : c0 + n] = value

            blur(est_x, s, 0, store_blurred)
            for index, (row, count, which) in enumerate(row_parts):
                if s == 0:
                    recorded = rec_ref[row : row + count, pl.ds(start, width)]
                else:
                    if it == 0:
                        rec_copy(s, index).wait()
                    recorded = rec_in[s, row : row + count, :]
                here = slice(rim + row, rim + row + count)
                quo[here, :] = recorded / quo[here, :]
                if which is not None:
                    rim_start(quo, 1 + s, which)
        for s in range(chips):
            quo = quo_x.at[s]
            rim_wait(quo, 1 + s)

            def store_log(c0, n, value):
                term = jnp.log(value)
                if s > 0:
                    term = acc[:, c0 : c0 + n] + term
                acc[:, c0 : c0 + n] = term

            blur(quo, s, 1, store_log)
        swap = pltpu.make_async_remote_copy(
            src_ref=acc,
            dst_ref=acc_in.at[it],
            send_sem=acc_send.at[it],
            recv_sem=acc_recv.at[it],
            device_id={"view": mate},
            device_id_type=MESH,
        )
        swap.start()
        swap.wait()
        if it < ITERS - 1:
            est_x[own, :] = est_x[own, :] * jnp.exp((acc[...] + acc_in[it]) / views)
            rim_start(est_x, 0, 0)
            rim_start(est_x, 0, 1)
        else:
            inner = pl.multiple_of(chip * part - start, LANE)
            mine = pl.ds(inner, part)
            there = pl.ds(pl.multiple_of(chip * part, LANE), part)
            out_ref[:, there] = est_x[own, mine] * jnp.exp(
                (acc[:, mine] + acc_in[it, :, mine]) / views
            )

    my_rows = pl.ds(pl.multiple_of(core * half, 8), half)

    def out_copy(step):
        columns = pl.ds(pl.multiple_of(chip * part, LANE), part)
        return pltpu.make_async_remote_copy(
            src_ref=out_ref.at[my_rows, columns],
            dst_ref=out_ref.at[my_rows, columns],
            send_sem=out_send.at[step],
            recv_sem=out_recv.at[step],
            device_id=peer(step),
            device_id_type=MESH,
        )

    def fwd_copy(step):
        columns = pl.ds(pl.multiple_of(chip_at(chips - step) * part, LANE), part)
        return pltpu.make_async_remote_copy(
            src_ref=out_ref.at[my_rows, columns],
            dst_ref=out_ref.at[my_rows, columns],
            send_sem=fwd_send.at[step],
            recv_sem=fwd_recv.at[step],
            device_id={"view": mate},
            device_id_type=MESH,
        )

    for step in range(1, chips):
        out_copy(step).start()
    for step in range(1, chips):
        out_copy(step).wait_recv()
        fwd_copy(step).start()
    for step in range(1, chips):
        out_copy(step).wait_send()
        fwd_copy(step).wait()


def local(tiles, views, recorded, psf_taps, estimate):
    nx, nz, ny = estimate.shape
    rows, rim = nx * nz, RADIUS * nz
    chips = views // CORES
    width = window_of(0, chips, ny)[1]
    vmem = pl.BlockSpec(memory_space=pltpu.VMEM)
    dma = pltpu.SemaphoreType.DMA
    parts = 3
    out = pl.pallas_call(
        functools.partial(body, nx, nz, ny, tiles, views),
        out_shape=jax.ShapeDtypeStruct((rows, ny), F32),
        in_specs=[vmem] * 3,
        out_specs=vmem,
        scratch_shapes=[
            pltpu.VMEM((rows + 2 * rim, width), F32),
            pltpu.VMEM((chips, rows + 2 * rim, width), F32),
            pltpu.VMEM((chips, rows, width), F32),
            pltpu.VMEM((rows, width), F32),
            pltpu.VMEM((ITERS, rows, width), F32),
            pltpu.VMEM((chips, 8, LANE), F32),
            pltpu.VMEM((chips, 2, rows, rows // 2 + 2 * rim), BF16),
            pltpu.VMEM((chips, 2, 2, 4 * LANE, 2 * LANE), BF16),
            pltpu.VMEM((rows, width + 2 * LANE), BF16),
            pltpu.VMEM((rows, width + 2 * LANE), BF16),
            dma((chips,)),
            dma((chips,)),
            dma((chips, parts)),
            dma((chips, parts)),
            dma((1 + chips, 2)),
            dma((1 + chips, 2)),
            dma((ITERS,)),
            dma((ITERS,)),
            dma((chips,)),
            dma((chips,)),
            dma((chips,)),
            dma((chips,)),
        ],
        compiler_params=pltpu.CompilerParams(
            collective_id=0, has_side_effects=True, vmem_limit_bytes=56 * 2**20
        ),
    )(recorded.reshape(rows, ny), psf_taps.reshape(3, TAPS), estimate.reshape(rows, ny))
    return out.reshape(estimate.shape)


def solution(mesh):
    in_specs = (P("view", "tile", "slab", None), P("view", None, None), P("tile", "slab", None))
    out_specs = P("tile", "slab", None)
    sizes = (mesh.shape["tile"], mesh.shape["view"])
    return jax.shard_map(
        functools.partial(local, *sizes),
        mesh=mesh, in_specs=in_specs, out_specs=out_specs, check_vma=False,
    )
```

```python
import functools

import jax
import jax.numpy as jnp
from jax import lax
from jax.experimental import pallas as pl
from jax.experimental.pallas import tpu as pltpu
from jax.sharding import PartitionSpec as P

RADIUS = 7
TAPS = 2 * RADIUS + 1
ITERS = 2
LANE = 128
CORES = 2
F32 = jnp.float32
BF16 = jnp.bfloat16
MESH = pl.DeviceIdType.MESH


def split(value):
    hi = value.astype(BF16)
    return hi, (value - hi.astype(F32)).astype(BF16)


def dot(a, b):
    return jnp.dot(a, b, preferred_element_type=F32)


def pieces(total, size):
    return [(start, min(size, total - start)) for start in range(0, total, size)]


def window_of(chip, chips, ny):
    part = ny // chips
    width = part + LANE * min(chips - 1, 2)
    start = jnp.clip(chip * part - LANE, 0, ny - width)
    return pl.multiple_of(start, LANE), width


def body(
    nx, nz, ny, tiles, views,
    rec_ref, taps_ref, est_ref, out_ref,
    est_x, quo_x, rec_in, acc, acc_in, kern, mat_xz, mat_y, u_hi, u_lo,
    kern_send, kern_recv, rec_send, rec_recv, rim_send, rim_recv,
    acc_send, acc_recv, out_send, out_recv, fwd_send, fwd_recv,
):
    chips = views // CORES
    part = ny // chips
    rows = nx * nz
    rim = RADIUS * nz
    half = rows // 2
    tile = lax.axis_index("tile")
    view = lax.axis_index("view")
    chip, core = view // CORES, view % CORES
    mate = chip * CORES + (1 - core)
    start, width = window_of(chip, chips, ny)
    own = slice(rim, rim + rows)
    chunks = pieces(width, 2 * LANE)

    def chip_at(step):
        return lax.rem(chip + step, chips)

    def peer(step):
        return {"view": chip_at(step) * CORES + core}

    barrier = pltpu.get_barrier_semaphore()
    for step in range(1, chips):
        pl.semaphore_signal(barrier, inc=1, device_id=peer(step), device_id_type=MESH)
    pl.semaphore_signal(barrier, inc=1, device_id={"view": mate}, device_id_type=MESH)

    @pl.when(tile > 0)
    def _():
        pl.semaphore_signal(barrier, inc=1, device_id={"tile": tile - 1}, device_id_type=MESH)

    @pl.when(tile < tiles - 1)
    def _():
        pl.semaphore_signal(barrier, inc=1, device_id={"tile": tile + 1}, device_id_type=MESH)

    taps = taps_ref[:, 0, :]
    kern[0, 0:3, 0:TAPS] = taps / jnp.sum(taps, axis=1, keepdims=True)
    est_x[own, :] = est_ref[:, pl.ds(start, width)]

    @pl.when(tile == 0)
    def _():
        est_x[0:rim, :] = jnp.zeros((rim, width), F32)
        for s in range(chips):
            quo_x[s, 0:rim, :] = jnp.zeros((rim, width), F32)

    @pl.when(tile == tiles - 1)
    def _():
        est_x[rim + rows :, :] = jnp.zeros((rim, width), F32)
        for s in range(chips):
            quo_x[s, rim + rows :, :] = jnp.zeros((rim, width), F32)

    tile_peers = jnp.minimum(tile, 1) + jnp.minimum(tiles - 1 - tile, 1)
    pl.semaphore_wait(barrier, chips + tile_peers)

    def rim_copy(array, number, index, which):
        c0, n = chunks[index]
        near, far, neighbour = ((rim, rim + rows, tile - 1), (rows, 0, tile + 1))[which]
        return pltpu.make_async_remote_copy(
            src_ref=array.at[pl.ds(near, rim), pl.ds(c0, n)],
            dst_ref=array.at[pl.ds(far, rim), pl.ds(c0, n)],
            send_sem=rim_send.at[number, index, which],
            recv_sem=rim_recv.at[number, index, which],
            device_id={"tile": neighbour},
            device_id_type=MESH,
        )

    def rim_start(array, number, index):
        @pl.when(tile > 0)
        def _():
            rim_copy(array, number, index, 0).start()

        @pl.when(tile < tiles - 1)
        def _():
            rim_copy(array, number, index, 1).start()

    def rim_wait(array, number, index):
        @pl.when(tile > 0)
        def _():
            rim_copy(array, number, index, 0).wait_send()
            rim_copy(array, number, index, 1).wait_recv()

        @pl.when(tile < tiles - 1)
        def _():
            rim_copy(array, number, index, 1).wait_send()
            rim_copy(array, number, index, 0).wait_recv()

    for index in range(len(chunks)):
        rim_start(est_x, 0, index)

    def kern_copy(step):
        return pltpu.make_async_remote_copy(
            src_ref=kern.at[0],
            dst_ref=kern.at[step],
            send_sem=kern_send.at[step],
            recv_sem=kern_recv.at[step],
            device_id=peer(chips - step),
            device_id_type=MESH,
        )

    def rec_copy(step, index):
        c0, n = chunks[index]
        begin, _ = window_of(chip_at(chips - step), chips, ny)
        return pltpu.make_async_remote_copy(
            src_ref=rec_ref.at[:, pl.ds(pl.multiple_of(begin + c0, LANE), n)],
            dst_ref=rec_in.at[step, :, pl.ds(c0, n)],
            send_sem=rec_send.at[step, index],
            recv_sem=rec_recv.at[step, index],
            device_id=peer(chips - step),
            device_id_type=MESH,
        )

    for step in range(1, chips):
        kern_copy(step).start()
        rec_copy(step, 0).start()

    def build(s):
        kern_s = kern[s]
        width_s = mat_xz.shape[-1]
        wide = -(-width_s // LANE) * LANE
        a = lax.broadcasted_iota(jnp.int32, (nz, wide), 0)
        column = lax.broadcasted_iota(jnp.int32, (nz, wide), 1)
        p, b = lax.div(column, jnp.int32(nz)), lax.rem(column, jnp.int32(nz))
        r = lax.broadcasted_iota(jnp.int32, (3 * LANE, LANE), 0)
        c = lax.broadcasted_iota(jnp.int32, (3 * LANE, LANE), 1)
        for mirrored in range(2):
            fx = jnp.zeros((nz, wide), F32)
            fz = jnp.zeros((nz, wide), F32)
            fy = jnp.zeros((3 * LANE, LANE), F32)
            for k in range(TAPS):
                o = TAPS - 1 - k if mirrored else k
                fx = jnp.where(p == k, kern_s[0:1, o : o + 1], fx)
                fz = jnp.where(b - a + RADIUS == k, kern_s[1:2, o : o + 1], fz)
                fy = jnp.where(r - c - LANE + RADIUS == k, kern_s[2:3, o : o + 1], fy)
            strip = fx * fz
            for i in range(nx // 2):
                moved = strip if i == 0 else pltpu.roll(strip, i * nz, 1)
                hi, lo = split(moved)
                mat_xz[s, mirrored, i * nz : (i + 1) * nz, :] = hi[:, :width_s]
                mat_xz[s, mirrored, half + i * nz : half + (i + 1) * nz, :] = lo[:, :width_s]
            for index, value in enumerate(split(fy)):
                mat_y[s, mirrored, index, 0 : 3 * LANE, 0:LANE] = value
                mat_y[s, mirrored, index, LANE : 4 * LANE, LANE : 2 * LANE] = value
                mat_y[s, mirrored, index, 3 * LANE :, 0:LANE] = jnp.zeros((LANE, LANE), BF16)
                mat_y[s, mirrored, index, 0:LANE, LANE : 2 * LANE] = jnp.zeros((LANE, LANE), BF16)

    for u in (u_hi, u_lo):
        u[:, 0:LANE] = jnp.zeros((rows, LANE), BF16)
        u[:, LANE + width :] = jnp.zeros((rows, LANE), BF16)

    def blur(source, s, mirrored, ready, store, between=None):
        depth = half + 2 * rim

        def along_xz(index):
            c0, n = chunks[index]
            for h in range(2):
                hi, lo = split(source[h * half : h * half + depth, c0 : c0 + n])
                both = dot(mat_xz[s, mirrored], hi)
                value = both[:half] + both[half:] + dot(mat_xz[s, mirrored, :half], lo)
                hi, lo = split(value)
                u_hi[h * half : (h + 1) * half, LANE + c0 : LANE + c0 + n] = hi
                u_lo[h * half : (h + 1) * half, LANE + c0 : LANE + c0 + n] = lo

        def along_y(index):
            c0, n = chunks[index]
            k = n + 2 * LANE
            hi, lo = u_hi[:, c0 : c0 + k], u_lo[:, c0 : c0 + k]
            m_hi, m_lo = mat_y[s, mirrored, 0, :k, :n], mat_y[s, mirrored, 1, :k, :n]
            store(index, dot(hi, m_hi) + dot(lo, m_hi) + dot(hi, m_lo))

        for index in range(len(chunks)):
            ready(index)
            along_xz(index)
            if index > 0:
                along_y(index - 1)
            if index == 0 and between is not None:
                between()
        along_y(len(chunks) - 1)

    def swap(it, index):
        c0, n = chunks[index]
        return pltpu.make_async_remote_copy(
            src_ref=acc.at[:, pl.ds(c0, n)],
            dst_ref=acc_in.at[it, :, pl.ds(c0, n)],
            send_sem=acc_send.at[it, index],
            recv_sem=acc_recv.at[it, index],
            device_id={"view": mate},
            device_id_type=MESH,
        )

    def second_recorded():
        for step in range(1, chips):
            rec_copy(step, 0).wait_send()
            if len(chunks) > 1:
                rec_copy(step, 1).start()

    def later_recorded():
        for step in range(1, chips):
            for index in range(2, len(chunks)):
                rec_copy(step, index).start()

    def forward(it, s):
        quo = quo_x.at[s]

        def ready(index):
            if s == 0:
                rim_wait(est_x, 0, index)

        def store_quotient(index, blurred):
            c0, n = chunks[index]
            if s == 0:
                recorded = rec_ref[:, pl.ds(pl.multiple_of(start + c0, LANE), n)]
            else:
                if it == 0:
                    rec_copy(s, index).wait_recv()
                    if index > 0:
                        rec_copy(s, index).wait_send()
                recorded = rec_in[s, :, c0 : c0 + n]
            quo[own, c0 : c0 + n] = recorded / blurred
            rim_start(quo, 1 + s, index)

        first = it == 0 and s == 0
        blur(est_x, s, 0, ready, store_quotient, second_recorded if first else None)
        if first:
            later_recorded()

    def backward(it, s):
        quo = quo_x.at[s]

        def ready(index):
            rim_wait(quo, 1 + s, index)

        def store_log(index, value):
            c0, n = chunks[index]
            term = jnp.log(value)
            if s > 0:
                term = acc[:, c0 : c0 + n] + term
            acc[:, c0 : c0 + n] = term
            if s == chips - 1:
                swap(it, index).start()

        blur(quo, s, 1, ready, store_log)

    my_rows = pl.ds(pl.multiple_of(core * half, 8), half)
    inner = pl.multiple_of(chip * part - start, LANE)
    out_parts = pieces(part, 2 * LANE)

    def gather_copy(step, index, forwarded):
        c0, n = out_parts[index]
        owner = chip_at(chips - step) if forwarded else chip
        place = (my_rows, pl.ds(pl.multiple_of(owner * part + c0, LANE), n))
        send, recv = (fwd_send, fwd_recv) if forwarded else (out_send, out_recv)
        return pltpu.make_async_remote_copy(
            src_ref=out_ref.at[place],
            dst_ref=out_ref.at[place],
            send_sem=send.at[step, index],
            recv_sem=recv.at[step, index],
            device_id={"view": mate} if forwarded else peer(step),
            device_id_type=MESH,
        )

    def finish(index, which):
        c0, n = out_parts[index]
        there = pl.ds(pl.multiple_of(chip * part + c0, LANE), n)
        here = pl.ds(pl.multiple_of(inner + c0, LANE), n)
        begin = pl.multiple_of((core if which == 0 else 1 - core) * half, 8)
        row = pl.ds(begin, half)
        total = acc[row, here] + acc_in[ITERS - 1, row, here]
        out_ref[row, there] = est_x[pl.ds(pl.multiple_of(rim + begin, 8), half), here] * jnp.exp(
            total / views
        )

    build(0)
    for it in range(ITERS):
        for s in range(chips):
            if it == 0 and s > 0:
                kern_copy(s).wait()
                build(s)
            forward(it, s)
        for s in range(chips):
            backward(it, s)
        if it < ITERS - 1:
            for index, (c0, n) in enumerate(chunks):
                swap(it, index).wait()
                here = slice(c0, c0 + n)
                est_x[own, here] = est_x[own, here] * jnp.exp(
                    (acc[:, here] + acc_in[it, :, here]) / views
                )
                rim_start(est_x, 0, index)

    done = 0
    for index, (c0, n) in enumerate(out_parts):
        while done < len(chunks) and chunks[done][0] < width - part + c0 + n:
            swap(ITERS - 1, done).wait()
            done += 1
        finish(index, 0)
        for step in range(1, chips):
            gather_copy(step, index, False).start()
    for index in range(len(out_parts)):
        finish(index, 1)
    for index in range(len(out_parts)):
        for step in range(1, chips):
            gather_copy(step, index, False).wait_recv()
            gather_copy(step, index, True).start()
    for index in range(len(out_parts)):
        for step in range(1, chips):
            gather_copy(step, index, False).wait_send()
            gather_copy(step, index, True).wait()


def local(tiles, views, recorded, psf_taps, estimate):
    nx, nz, ny = estimate.shape
    rows, rim = nx * nz, RADIUS * nz
    chips = views // CORES
    width = window_of(0, chips, ny)[1]
    vmem = pl.BlockSpec(memory_space=pltpu.VMEM)
    dma = pltpu.SemaphoreType.DMA
    parts = len(pieces(width, 2 * LANE))
    outs = len(pieces(ny // chips, 2 * LANE))
    out = pl.pallas_call(
        functools.partial(body, nx, nz, ny, tiles, views),
        out_shape=jax.ShapeDtypeStruct((rows, ny), F32),
        in_specs=[vmem] * 3,
        out_specs=vmem,
        scratch_shapes=[
            pltpu.VMEM((rows + 2 * rim, width), F32),
            pltpu.VMEM((chips, rows + 2 * rim, width), F32),
            pltpu.VMEM((chips, rows, width), F32),
            pltpu.VMEM((rows, width), F32),
            pltpu.VMEM((ITERS, rows, width), F32),
            pltpu.VMEM((chips, 8, LANE), F32),
            pltpu.VMEM((chips, 2, rows, rows // 2 + 2 * rim), BF16),
            pltpu.VMEM((chips, 2, 2, 4 * LANE, 2 * LANE), BF16),
            pltpu.VMEM((rows, width + 2 * LANE), BF16),
            pltpu.VMEM((rows, width + 2 * LANE), BF16),
            dma((chips,)),
            dma((chips,)),
            dma((chips, parts)),
            dma((chips, parts)),
            dma((1 + chips, parts, 2)),
            dma((1 + chips, parts, 2)),
            dma((ITERS, parts)),
            dma((ITERS, parts)),
            dma((chips, outs)),
            dma((chips, outs)),
            dma((chips, outs)),
            dma((chips, outs)),
        ],
        compiler_params=pltpu.CompilerParams(
            collective_id=0, has_side_effects=True, vmem_limit_bytes=56 * 2**20
        ),
    )(recorded.reshape(rows, ny), psf_taps.reshape(3, 1, TAPS), estimate.reshape(rows, ny))
    return out.reshape(estimate.shape)


def solution(mesh):
    in_specs = (P("view", "tile", "slab", None), P("view", None, None), P("tile", "slab", None))
    out_specs = P("tile", "slab", None)
    sizes = (mesh.shape["tile"], mesh.shape["view"])
    return jax.shard_map(
        functools.partial(local, *sizes),
        mesh=mesh, in_specs=in_specs, out_specs=out_specs, check_vma=False,
    )
```
